32 devices in a mesh: gx: 8 (over z, core), gy: 4 (over y, x).
Axes of the slice: x: 2, y: 2, z: 4, core: 2. Of those that a mesh axis runs over, the one named last changes fastest.
Arguments:
- forcing: float32 [4, 8, 2048, 512], P(None, None, 'gx', 'gy'), may hold values from -150 to 150
- velocity: float32 [2, 2048, 512], P(None, 'gx', 'gy'), may hold values from -0.6 to 0.6
- viscosity: float32 [2048, 512], P('gx', 'gy'), may hold values from 0.05 to 0.25
- sound: float32 [2048, 512], P('gx', 'gy'), may hold values from 0.4 to 1
- coupling: float32 [4, 4, 2048, 512], P(None, None, 'gx', 'gy'), may hold values from -1.5 to 1.5
Outputs:
- basis: float32 [4, 8, 2048, 512], P(None, None, 'gx', 'gy')
- factor: float32 [8, 8], replicated
The draws below stay inside these ranges and needn't reach their ends.
All inputs are finite; a program needn't handle non-finite values.
Results may differ from the reference program's by a relative error of at most 0.000055.
Values sent between devices are 32-bit elements; how exact they have to be, the bound alone decides.
A program may use at most 128 MiB of HBM per device.

```python
import math
import jax
import jax.numpy as jnp
from jax import lax

NVAR = 4
NCOL = 8
NX = 2048
NY = 512
ROWS = 4194304


def draw_forcing(key, part):
    key_base, key_rough, key_cols = jax.random.split(key, 3)
    xs = jnp.arange(NX, dtype=jnp.float32) / NX
    ys = jnp.arange(NY, dtype=jnp.float32) / NY
    base = jnp.clip(jax.random.normal(key_base, (NVAR, NCOL, NX, NY), jnp.float32), -5.0, 5.0)
    envelope = jnp.exp(0.55 * xs)[:, None] * jnp.exp(0.55 * ys)[None, :]
    rough = jnp.exp(jax.random.uniform(key_rough, (NX, NY), jnp.float32, 0.0, 1.2))
    col_scale = jnp.exp(jax.random.uniform(key_cols, (NCOL,), jnp.float32, 0.0, 1.1))
    return (base * col_scale[None, :, None, None] * (envelope * rough)[None, None]).astype(jnp.float32)


def shard_levels(key, dims, pieces, least, high):
    def one(dim, parts):
        heights = jax.random.uniform(jax.random.fold_in(jax.random.fold_in(key, 6), dim), (parts,), jnp.float32, least / len(pieces), high / len(pieces))
        return jnp.repeat(jnp.exp(heights), dims[dim] // parts).reshape((-1,) + (1,) * (len(dims) - dim - 1))

    factor_of = one(*pieces[0])
    for cut in pieces[1:]:
        factor_of = factor_of * one(*cut)
    return factor_of


def centred(rng, shape, deviation, reach, cuts=(), kind=jnp.bfloat16):
    gain = shard_levels(rng, shape, cuts, -0.22, 0.18) if cuts else 1.0
    values = jax.random.normal(rng, shape, jnp.float32) * deviation * gain
    return jnp.minimum(jnp.maximum(values, -reach), reach).astype(kind)


def setup_inputs(seed: int = 0) -> dict:
    key_of = jax.random.split(jax.random.key(seed), 6)
    forcing = draw_forcing(jax.random.fold_in(key_of[5], 71), 0)
    velocity = jnp.clip(jax.random.uniform(key_of[1], (2, NX, NY), jnp.float32, -0.6, 0.6) * shard_levels(key_of[1], (2, NX, NY), ((1, 8), (2, 4)), -0.4, 0.0), -0.6, 0.6)
    viscosity = jnp.clip(jnp.exp(math.log(0.25) - 1.609438 * jax.random.uniform(key_of[2], (NX, NY), jnp.float32) ** shard_levels(key_of[2], (NX, NY), ((0, 8), (1, 4)), -0.2, 0.2)), 0.05, 0.25)
    sound = jnp.clip(jnp.exp(math.log(1.0) - 0.9162907 * jax.random.uniform(key_of[3], (NX, NY), jnp.float32) ** shard_levels(key_of[3], (NX, NY), ((0, 8), (1, 4)), -0.2, 0.2)), 0.4, 1.0)
    coupling = centred(key_of[4], (NVAR, NVAR, NX, NY), 0.3, 1.5, ((2, 8), (3, 4)), jnp.float32)
    return {"forcing": forcing, "velocity": velocity, "viscosity": viscosity, "sound": sound, "coupling": coupling}


STEP = 0.5

def tendency(padded, velocity, viscosity, sound, coupling):
    center = padded[:, :, 1:-1, 1:-1]
    east = padded[:, :, 2:, 1:-1]
    west = padded[:, :, :-2, 1:-1]
    north = padded[:, :, 1:-1, 2:]
    south = padded[:, :, 1:-1, :-2]
    grad_x = 0.5 * (east - west)
    grad_y = 0.5 * (north - south)
    laplace = east + west + north + south - 4.0 * center
    transport = viscosity * laplace - velocity[0] * grad_x - velocity[1] * grad_y
    divergence = grad_x[1] + grad_y[2]
    acoustic = jnp.stack([-sound * divergence, -sound * grad_x[3], -sound * grad_y[3], -sound * divergence])
    mixing = coupling[:, 0][:, None] * center[0][None]
    for inner in range(1, 4):
        mixing = mixing + coupling[:, inner][:, None] * center[inner][None]
    return transport + acoustic - mixing

def pad_one(field):
    return jnp.pad(field, ((0, 0), (0, 0), (1, 1), (1, 1)))

def advance(state, velocity, viscosity, sound, coupling):
    first = tendency(pad_one(state), velocity, viscosity, sound, coupling) + state
    middle = state + STEP * first
    second = tendency(pad_one(middle), velocity, viscosity, sound, coupling) + state
    return state + 0.5 * STEP * (first + second)

def reference(forcing, velocity, viscosity, sound, coupling):
    columns = jnp.moveaxis(forcing, 1, 0)

    def one_column(column):
        return advance(column[:, None], velocity, viscosity, sound, coupling)[:, 0]
    response = jnp.moveaxis(lax.map(one_column, columns), 0, 1)
    gram = jnp.einsum('vcxy,vdxy->cd', response, response, precision=lax.Precision.HIGHEST) / ROWS
    lower = jnp.linalg.cholesky(gram)
    identity = jnp.eye(NCOL, dtype=lower.dtype)
    inverse = lax.linalg.triangular_solve(lower, identity, left_side=True, lower=True)
    basis = jnp.einsum('cd,vdxy->vcxy', inverse, response, precision=lax.Precision.HIGHEST)
    return (basis, lower.T)
```

```python
import functools

import jax
import jax.numpy as jnp
from jax import lax
from jax.experimental import pallas as pl
from jax.experimental.pallas import tpu as pltpu
from jax.sharding import PartitionSpec as P

MESH = pl.DeviceIdType.MESH
NV = 4
NC = 8
GROUPS = 2
CG = NC // GROUPS
NF = NV * CG
PAIRS = [(i, j) for i in range(NC) for j in range(i + 1)]
PAIR_INDEX = {p: k for k, p in enumerate(PAIRS)}
PADDED_PAIRS = 40
KE, KW, KN, KS, KA, KM = 0, 1, 2, 3, 4, 5
KD = KM + NV * NV
NK = KD + NV


def response_kernel(
    nx, ny, f_hbm, vel_hbm, visc_hbm, sound_hbm, coup_hbm,
    r_hbm, gram_ref,
    fbuf, mbuf, rbuf, coef, halo, pack, tpose,
    vel, visc, sound, coup, acc, gx_slots, gy_slots,
    row_send, row_recv, col_send, col_recv,
    in_sem, out_sem, rs_sem, rr_sem, cs_sem, cr_sem, g1_send, g1_recv, g2_send, g2_recv,
):
    rows = f_hbm.shape[2]
    chunks = rows // 8
    halves = rows // 128
    gx, gy = lax.axis_index("gx"), lax.axis_index("gy")

    def cols(ref, g):
        return ref.at[:, pl.ds(g * CG, CG)]

    loads = []
    for g in range(GROUPS):
        loads.append(pltpu.make_async_copy(
            cols(f_hbm, g), fbuf.at[:, pl.ds(g * CG, CG), pl.ds(8, rows)], in_sem.at[g]))
    coef_loads = [
        pltpu.make_async_copy(a, b, in_sem.at[GROUPS + k])
        for k, (a, b) in enumerate(
            [(vel_hbm, vel), (visc_hbm, visc), (sound_hbm, sound), (coup_hbm, coup)])
    ]
    for cp in loads + coef_loads:
        cp.start()

    barrier = pltpu.get_barrier_semaphore()
    for r in range(1, nx):
        pl.semaphore_signal(barrier, inc=1, device_id=(lax.rem(gx + r, nx), gy), device_id_type=MESH)
    for r in range(1, ny):
        pl.semaphore_signal(barrier, inc=1, device_id=(gx, lax.rem(gy + r, ny)), device_id_type=MESH)

    def zero_side(ref, side):
        for s in range(2):
            for g in range(GROUPS):
                ref[s, g, side] = jnp.zeros(ref.shape[3:], jnp.float32)

    pl.when(gx == 0)(lambda: zero_side(row_recv, 0))
    pl.when(gx == nx - 1)(lambda: zero_side(row_recv, 1))
    pl.when(gy == 0)(lambda: zero_side(col_recv, 0))
    pl.when(gy == ny - 1)(lambda: zero_side(col_recv, 1))

    lane = lax.broadcasted_iota(jnp.int32, (8, 128), 1)
    first_lane = lane == 0
    last_lane = lane == 127

    def row_copy(s, g, up):
        return pltpu.make_async_remote_copy(
            src_ref=row_send.at[s, g, up], dst_ref=row_recv.at[s, g, 1 - up],
            send_sem=rs_sem.at[s, g, up], recv_sem=rr_sem.at[s, g, 1 - up],
            device_id=(gx + (1 if up else -1), gy), device_id_type=MESH)

    def col_copy(s, g, up):
        return pltpu.make_async_remote_copy(
            src_ref=col_send.at[s, g, up], dst_ref=col_recv.at[s, g, 1 - up],
            send_sem=cs_sem.at[s, g, up], recv_sem=cr_sem.at[s, g, 1 - up],
            device_id=(gx, gy + (1 if up else -1)), device_id_type=MESH)

    def send(s, g, src):
        for v in range(NV):
            for cl in range(CG):
                k = v * CG + cl
                row_send[s, g, 0, k:k + 1, :] = src[v, g * CG + cl, 8:9, :]
                row_send[s, g, 1, k:k + 1, :] = src[v, g * CG + cl, 7 + rows:8 + rows, :]
        for h in range(halves):
            tpose[...] = pack[h * 128:(h + 1) * 128, :].T
            col_send[s, g, 1, h * NF:(h + 1) * NF, :] = tpose[pl.ds(0, NF, stride=2), :]
            col_send[s, g, 0, h * NF:(h + 1) * NF, :] = tpose[pl.ds(1, NF, stride=2), :]

    def launch(s, g):
        pl.when(gx > 0)(lambda: row_copy(s, g, 0).start())
        pl.when(gx < nx - 1)(lambda: row_copy(s, g, 1).start())
        pl.when(gy > 0)(lambda: col_copy(s, g, 0).start())
        pl.when(gy < ny - 1)(lambda: col_copy(s, g, 1).start())

    def receive(s, g, dst):
        pl.when(gx > 0)(lambda: row_copy(s, g, 1).wait_recv())
        pl.when(gx < nx - 1)(lambda: row_copy(s, g, 0).wait_recv())
        pl.when(gy > 0)(lambda: col_copy(s, g, 1).wait_recv())
        pl.when(gy < ny - 1)(lambda: col_copy(s, g, 0).wait_recv())
        for v in range(NV):
            for cl in range(CG):
                k = v * CG + cl
                dst[v, g * CG + cl, 7:8, :] = row_recv[s, g, 0, k:k + 1, :]
                dst[v, g * CG + cl, 8 + rows:9 + rows, :] = row_recv[s, g, 1, k:k + 1, :]
        for h in range(halves):
            tpose[pl.ds(0, NF, stride=2), :] = col_recv[s, g, 1, h * NF:(h + 1) * NF, :]
            tpose[pl.ds(1, NF, stride=2), :] = col_recv[s, g, 0, h * NF:(h + 1) * NF, :]
            halo[h * 128:(h + 1) * 128, :] = tpose[...].T

    def finish_sends(s, g):
        pl.when(gx > 0)(lambda: row_copy(s, g, 0).wait_send())
        pl.when(gx < nx - 1)(lambda: row_copy(s, g, 1).wait_send())
        pl.when(gy > 0)(lambda: col_copy(s, g, 0).wait_send())
        pl.when(gy < ny - 1)(lambda: col_copy(s, g, 1).wait_send())

    def packed(total, value, k):
        return jnp.where((lane == 2 * k) | (lane == 2 * k + 1), pltpu.roll(value, 2 * k + 1, 1), total)

    def pack_input(g):
        def body(i, _):
            at = pl.multiple_of(i * 8, 8)
            total = jnp.zeros((8, 128), jnp.float32)
            for v in range(NV):
                for cl in range(CG):
                    value = fbuf[v, g * CG + cl, pl.ds(at + 8, 8), :]
                    total = packed(total, value, v * CG + cl)
            pack[pl.ds(at, 8), :] = total
            return 0
        lax.fori_loop(0, chunks, body, 0, unroll=4)

    def operator(src, g, cl, at, ks, edges, first):
        q, d1, d2, out = [], {}, {}, []
        for v in range(NV):
            c = g * CG + cl
            mid = src[v, c, pl.ds(at + 8, 8), :]
            east = src[v, c, pl.ds(at + 9, 8), :]
            west = src[v, c, pl.ds(at + 7, 8), :]
            edge = pltpu.roll(edges, 127 - 2 * (v * CG + cl), 1)
            north = jnp.where(last_lane, edge, pltpu.roll(mid, 127, 1))
            south = jnp.where(first_lane, edge, pltpu.roll(mid, 1, 1))
            q.append(mid)
            if v in (1, 3):
                d1[v] = east - west
            if v in (2, 3):
                d2[v] = north - south
            out.append((ks[KE] * east + ks[KW] * west) + (ks[KN] * north + ks[KS] * south))
        for w in range(NV):
            m = [ks[KD + v if first and v == w else KM + w * NV + v] * q[v] for v in range(NV)]
            out[w] = out[w] + ((m[0] + m[1]) + (m[2] + m[3]))
        div = ks[KA] * (d1[1] + d2[2])
        out[0] = out[0] - div
        out[1] = out[1] - ks[KA] * d1[3]
        out[2] = out[2] - ks[KA] * d2[3]
        out[3] = out[3] - div
        return out

    def stage_one(g):
        def body(i, _):
            at = pl.multiple_of(i * 8, 8)
            ks = [coef[k, pl.ds(at, 8), :] for k in range(NK)]
            edges = halo[pl.ds(at, 8), :]
            total = jnp.zeros((8, 128), jnp.float32)
            for cl in range(CG):
                middle = operator(fbuf, g, cl, at, ks, edges, True)
                for v in range(NV):
                    mbuf[v, g * CG + cl, pl.ds(at + 8, 8), :] = middle[v]
                    total = packed(total, middle[v], v * CG + cl)
            pack[pl.ds(at, 8), :] = total
            return 0
        lax.fori_loop(0, chunks, body, 0, unroll=2)

    def stage_two(g):
        def body(i, _):
            at = pl.multiple_of(i * 8, 8)
            ks = [coef[k, pl.ds(at, 8), :] for k in range(NK)]
            edges = halo[pl.ds(at, 8), :]
            res = {}
            for cl in range(CG):
                c = g * CG + cl
                out = operator(mbuf, g, cl, at, ks, edges, False)
                for v in range(NV):
                    value = 1.5 * fbuf[v, c, pl.ds(at + 8, 8), :] + out[v]
                    rbuf[v, c, pl.ds(at, 8), :] = value
                    res[v, c] = value
            for c in range(g * CG):
                for v in range(NV):
                    res[v, c] = rbuf[v, c, pl.ds(at, 8), :]
            for c in range(g * CG, (g + 1) * CG):
                for d in range(c + 1):
                    p = [res[v, c] * res[v, d] for v in range(NV)]
                    acc[PAIR_INDEX[c, d]] += (p[0] + p[1]) + (p[2] + p[3])
            return 0
        lax.fori_loop(0, chunks, body, 0, unroll=2)

    def r_copy(g):
        return pltpu.make_async_copy(cols(rbuf, g), cols(r_hbm, g), out_sem.at[g])

    for g in range(GROUPS):
        loads[g].wait()
        pack_input(g)
        send(0, g, fbuf)
        if g == 0:
            pl.semaphore_wait(barrier, nx + ny - 2)
        launch(0, g)
    acc[...] = jnp.zeros_like(acc)
    for cp in coef_loads:
        cp.wait()

    def fold(i, _):
        at = pl.multiple_of(i * 8, 8)
        half = 0.5 * visc[pl.ds(at, 8), :]
        vx = 0.25 * vel[0, pl.ds(at, 8), :]
        vy = 0.25 * vel[1, pl.ds(at, 8), :]
        coef[KE, pl.ds(at, 8), :] = half - vx
        coef[KW, pl.ds(at, 8), :] = half + vx
        coef[KN, pl.ds(at, 8), :] = half - vy
        coef[KS, pl.ds(at, 8), :] = half + vy
        coef[KA, pl.ds(at, 8), :] = 0.25 * sound[pl.ds(at, 8), :]
        for w in range(NV):
            for v in range(NV):
                k = -0.5 * coup[w, v, pl.ds(at, 8), :]
                if v == w:
                    coef[KD + v, pl.ds(at, 8), :] = k + (1.5 - 4.0 * half)
                    k = k + (1.0 - 4.0 * half)
                coef[KM + w * NV + v, pl.ds(at, 8), :] = k
        return 0
    lax.fori_loop(0, chunks, fold, 0)

    for g in range(GROUPS):
        receive(0, g, fbuf)
        stage_one(g)
        send(1, g, mbuf)
        launch(1, g)
    for g in range(GROUPS):
        receive(1, g, mbuf)
        stage_two(g)
        r_copy(g).start()

    scale = 0.25 / float(NV * rows * 128 * nx * ny)
    lanes = jnp.sum(jnp.sum(acc[...], axis=1), axis=1, keepdims=True)
    spot = lax.broadcasted_iota(jnp.int32, (PADDED_PAIRS, 128), 1) == lax.broadcasted_iota(
        jnp.int32, (PADDED_PAIRS, 128), 0)
    line = jnp.sum(jnp.where(spot, lanes, 0.0), axis=0, keepdims=True) * scale
    gx_slots[gx] = jnp.broadcast_to(line, (8, 128))

    def gx_copy(r, owner):
        return pltpu.make_async_remote_copy(
            src_ref=gx_slots.at[owner], dst_ref=gx_slots.at[owner],
            send_sem=g1_send.at[r], recv_sem=g1_recv.at[owner],
            device_id=(lax.rem(gx + r, nx), gy), device_id_type=MESH)

    def gy_copy(r, owner):
        return pltpu.make_async_remote_copy(
            src_ref=gy_slots.at[owner], dst_ref=gy_slots.at[owner],
            send_sem=g2_send.at[r], recv_sem=g2_recv.at[owner],
            device_id=(gx, lax.rem(gy + r, ny)), device_id_type=MESH)

    for r in range(1, nx):
        gx_copy(r, gx).start()
    for r in range(1, nx):
        gx_copy(r, lax.rem(gx + nx - r, nx)).wait_recv()
    gy_slots[gy] = functools.reduce(jnp.add, [gx_slots[k] for k in range(nx)])
    for r in range(1, ny):
        gy_copy(r, gy).start()
    for r in range(1, ny):
        gy_copy(r, lax.rem(gy + ny - r, ny)).wait_recv()
    gram_ref[...] = functools.reduce(jnp.add, [gy_slots[k] for k in range(ny)])

    for r in range(1, nx):
        gx_copy(r, gx).wait_send()
    for r in range(1, ny):
        gy_copy(r, gy).wait_send()
    for s in range(2):
        for g in range(GROUPS):
            finish_sends(s, g)
    for g in range(GROUPS):
        r_copy(g).wait()


def basis_kernel(gram_ref, r_ref, basis_ref, factor_ref, inv_ref):
    @pl.when((pl.program_id(0) == 0) & (pl.program_id(1) == 0))
    def _():
        gram = {p: jnp.broadcast_to(gram_ref[:, k:k + 1], (8, 128)) for k, p in enumerate(PAIRS)}
        low, inv, diag = {}, {}, {}
        for j in range(NC):
            for i in range(j, NC):
                s = gram[i, j]
                for k in range(j):
                    s = s - low[i, k] * low[j, k]
                if i == j:
                    r = lax.rsqrt(s)
                    r = r * (1.5 - 0.5 * s * r * r)
                    diag[j] = r
                    low[j, j] = s * r
                else:
                    low[i, j] = s * diag[j]
        for j in range(NC):
            inv[j, j] = diag[j]
            for i in range(j + 1, NC):
                s = low[i, j] * inv[j, j]
                for k in range(j + 1, i):
                    s = s + low[i, k] * inv[k, j]
                inv[i, j] = -diag[i] * s
        row = lax.broadcasted_iota(jnp.int32, (8, 128), 0)
        lane = lax.broadcasted_iota(jnp.int32, (8, 128), 1)
        factor = jnp.zeros((8, 128), jnp.float32)
        for k, (i, j) in enumerate(PAIRS):
            factor = jnp.where((row == j) & (lane == i), low[i, j], factor)
            inv_ref[k] = 0.5 * inv[i, j]
        factor_ref[...] = factor[:, :NC]

    inv = [inv_ref[k] for k in range(len(PAIRS))]

    def body(i, _):
        at = pl.multiple_of(i * 8, 8)
        r = [r_ref[0, c, pl.ds(at, 8), :] for c in range(NC)]
        for c in range(NC):
            total = inv[PAIR_INDEX[c, 0]] * r[0]
            for d in range(1, c + 1):
                total = total + inv[PAIR_INDEX[c, d]] * r[d]
            basis_ref[0, c, pl.ds(at, 8), :] = total
        return 0
    lax.fori_loop(0, r_ref.shape[2] // 8, body, 0, unroll=2)


def local(nx, ny, forcing, velocity, viscosity, sound, coupling):
    rows = forcing.shape[2]
    f32 = jnp.float32
    hbm = pl.BlockSpec(memory_space=pl.ANY)
    vmem = pl.BlockSpec(memory_space=pltpu.VMEM)
    dma = pltpu.SemaphoreType.DMA
    response, gram = pl.pallas_call(
        functools.partial(response_kernel, nx, ny),
        out_shape=(jax.ShapeDtypeStruct(forcing.shape, f32), jax.ShapeDtypeStruct((8, 128), f32)),
        in_specs=[pl.BlockSpec(memory_space=pltpu.HBM)] * 5,
        out_specs=(hbm, vmem),
        scratch_shapes=[
            pltpu.VMEM((NV, NC, rows + 16, 128), f32),
            pltpu.VMEM((NV, NC, rows + 16, 128), f32),
            pltpu.VMEM((NV, NC, rows, 128), f32),
            pltpu.VMEM((NK, rows, 128), f32),
            pltpu.VMEM((rows, 128), f32),
            pltpu.VMEM((rows, 128), f32),
            pltpu.VMEM((128, 128), f32),
            pltpu.VMEM(velocity.shape, f32),
            pltpu.VMEM(viscosity.shape, f32),
            pltpu.VMEM(sound.shape, f32),
            pltpu.VMEM(coupling.shape, f32),
            pltpu.VMEM((PADDED_PAIRS, 8, 128), f32),
            pltpu.VMEM((nx, 8, 128), f32),
            pltpu.VMEM((ny, 8, 128), f32),
            pltpu.VMEM((2, GROUPS, 2, NF, 128), f32),
            pltpu.VMEM((2, GROUPS, 2, NF, 128), f32),
            pltpu.VMEM((2, GROUPS, 2, rows // 128 * NF, 128), f32),
            pltpu.VMEM((2, GROUPS, 2, rows // 128 * NF, 128), f32),
            dma((GROUPS + 4,)), dma((GROUPS,)),
            dma((2, GROUPS, 2)), dma((2, GROUPS, 2)), dma((2, GROUPS, 2)), dma((2, GROUPS, 2)),
            dma((nx,)), dma((nx,)), dma((ny,)), dma((ny,)),
        ],
        compiler_params=pltpu.CompilerParams(
            collective_id=0, has_side_effects=True, vmem_limit_bytes=40 * 2**20),
        name="response",
    )(forcing, velocity, viscosity, sound, coupling)
    block = pl.BlockSpec((1, NC, rows // 2, 128), lambda v, i: (v, 0, i, 0))
    return tuple(pl.pallas_call(
        basis_kernel,
        grid=(NV, 2),
        out_shape=(jax.ShapeDtypeStruct(forcing.shape, f32), jax.ShapeDtypeStruct((NC, NC), f32)),
        in_specs=[pl.BlockSpec((8, 128), lambda v, i: (0, 0)), block],
        out_specs=(block, pl.BlockSpec((NC, NC), lambda v, i: (0, 0))),
        scratch_shapes=[pltpu.VMEM((len(PAIRS), 8, 128), f32)],
        compiler_params=pltpu.CompilerParams(vmem_limit_bytes=16 * 2**20),
        name="basis",
    )(gram, response))


def solution(mesh):
    in_specs = (
        P(None, None, "gx", "gy"),
        P(None, "gx", "gy"),
        P("gx", "gy"),
        P("gx", "gy"),
        P(None, None, "gx", "gy"),
    )
    out_specs = (P(None, None, "gx", "gy"), P())
    body = functools.partial(local, mesh.shape["gx"], mesh.shape["gy"])
    return jax.shard_map(body, mesh=mesh, in_specs=in_specs, out_specs=out_specs, check_vma=False)
```

```python
import functools

import jax
import jax.numpy as jnp
from jax import lax
from jax.experimental import pallas as pl
from jax.experimental.pallas import tpu as pltpu
from jax.sharding import PartitionSpec as P

MESH = pl.DeviceIdType.MESH
NV = 4
NC = 8
GROUPS = 2
CG = NC // GROUPS
NF = NV * CG
PAIRS = [(i, j) for i in range(NC) for j in range(i + 1)]
PAIR_INDEX = {p: k for k, p in enumerate(PAIRS)}
PADDED_PAIRS = 40
KE, KW, KN, KS, KA, KM = 0, 1, 2, 3, 4, 5
KD = KM + NV * NV
NK = KD + NV


def response_kernel(
    nx, ny, f_hbm, vel_hbm, visc_hbm, sound_hbm, coup_hbm,
    r_hbm, gram_ref,
    fbuf, mbuf, rbuf, coef, halo, pack, tpose,
    vel, visc, sound, coup, acc, gx_slots, gy_slots,
    row_send, row_recv, col_send, col_recv,
    in_sem, out_sem, rs_sem, rr_sem, cs_sem, cr_sem, g1_send, g1_recv, g2_send, g2_recv,
):
    rows = f_hbm.shape[2]
    chunks = rows // 8
    halves = rows // 128
    gx, gy = lax.axis_index("gx"), lax.axis_index("gy")

    def cols(ref, g):
        return ref.at[:, pl.ds(g * CG, CG)]

    loads = []
    for g in range(GROUPS):
        loads.append(pltpu.make_async_copy(
            cols(f_hbm, g), fbuf.at[:, pl.ds(g * CG, CG), pl.ds(8, rows)], in_sem.at[g]))
    coef_loads = [
        pltpu.make_async_copy(a, b, in_sem.at[GROUPS + k])
        for k, (a, b) in enumerate(
            [(vel_hbm, vel), (visc_hbm, visc), (sound_hbm, sound), (coup_hbm, coup)])
    ]
    for cp in loads + coef_loads:
        cp.start()

    barrier = pltpu.get_barrier_semaphore()
    for r in range(1, nx):
        pl.semaphore_signal(barrier, inc=1, device_id=(lax.rem(gx + r, nx), gy), device_id_type=MESH)
    for r in range(1, ny):
        pl.semaphore_signal(barrier, inc=1, device_id=(gx, lax.rem(gy + r, ny)), device_id_type=MESH)

    def zero_side(ref, side):
        for s in range(2):
            for g in range(GROUPS):
                ref[s, g, side] = jnp.zeros(ref.shape[3:], jnp.float32)

    pl.when(gx == 0)(lambda: zero_side(row_recv, 0))
    pl.when(gx == nx - 1)(lambda: zero_side(row_recv, 1))
    pl.when(gy == 0)(lambda: zero_side(col_recv, 0))
    pl.when(gy == ny - 1)(lambda: zero_side(col_recv, 1))

    lane = lax.broadcasted_iota(jnp.int32, (8, 128), 1)
    first_lane = lane == 0
    last_lane = lane == 127

    def row_copy(s, g, up):
        return pltpu.make_async_remote_copy(
            src_ref=row_send.at[s, g, up], dst_ref=row_recv.at[s, g, 1 - up],
            send_sem=rs_sem.at[s, g, up], recv_sem=rr_sem.at[s, g, 1 - up],
            device_id=(gx + (1 if up else -1), gy), device_id_type=MESH)

    def col_copy(s, g, up):
        return pltpu.make_async_remote_copy(
            src_ref=col_send.at[s, g, up], dst_ref=col_recv.at[s, g, 1 - up],
            send_sem=cs_sem.at[s, g, up], recv_sem=cr_sem.at[s, g, 1 - up],
            device_id=(gx, gy + (1 if up else -1)), device_id_type=MESH)

    def send(s, g, src):
        for v in range(NV):
            for cl in range(CG):
                k = v * CG + cl
                row_send[s, g, 0, k:k + 1, :] = src[v, g * CG + cl, 8:9, :]
                row_send[s, g, 1, k:k + 1, :] = src[v, g * CG + cl, 7 + rows:8 + rows, :]
        for h in range(halves):
            tpose[...] = pack[h * 128:(h + 1) * 128, :].T
            col_send[s, g, 1, h * NF:(h + 1) * NF, :] = tpose[pl.ds(0, NF, stride=2), :]
            col_send[s, g, 0, h * NF:(h + 1) * NF, :] = tpose[pl.ds(1, NF, stride=2), :]

    def launch(s, g):
        pl.when(gx > 0)(lambda: row_copy(s, g, 0).start())
        pl.when(gx < nx - 1)(lambda: row_copy(s, g, 1).start())
        pl.when(gy > 0)(lambda: col_copy(s, g, 0).start())
        pl.when(gy < ny - 1)(lambda: col_copy(s, g, 1).start())

    def receive(s, g, dst):
        pl.when(gx > 0)(lambda: row_copy(s, g, 1).wait_recv())
        pl.when(gx < nx - 1)(lambda: row_copy(s, g, 0).wait_recv())
        pl.when(gy > 0)(lambda: col_copy(s, g, 1).wait_recv())
        pl.when(gy < ny - 1)(lambda: col_copy(s, g, 0).wait_recv())
        for v in range(NV):
            for cl in range(CG):
                k = v * CG + cl
                dst[v, g * CG + cl, 7:8, :] = row_recv[s, g, 0, k:k + 1, :]
                dst[v, g * CG + cl, 8 + rows:9 + rows, :] = row_recv[s, g, 1, k:k + 1, :]
        for h in range(halves):
            tpose[pl.ds(0, NF, stride=2), :] = col_recv[s, g, 1, h * NF:(h + 1) * NF, :]
            tpose[pl.ds(1, NF, stride=2), :] = col_recv[s, g, 0, h * NF:(h + 1) * NF, :]
            halo[h * 128:(h + 1) * 128, :] = tpose[...].T

    def finish_sends(s, g):
        pl.when(gx > 0)(lambda: row_copy(s, g, 0).wait_send())
        pl.when(gx < nx - 1)(lambda: row_copy(s, g, 1).wait_send())
        pl.when(gy > 0)(lambda: col_copy(s, g, 0).wait_send())
        pl.when(gy < ny - 1)(lambda: col_copy(s, g, 1).wait_send())

    def packed(total, value, k):
        return jnp.where((lane == 2 * k) | (lane == 2 * k + 1), pltpu.roll(value, 2 * k + 1, 1), total)

    def pack_input(g):
        def body(i, _):
            at = pl.multiple_of(i * 8, 8)
            total = jnp.zeros((8, 128), jnp.float32)
            for v in range(NV):
                for cl in range(CG):
                    value = fbuf[v, g * CG + cl, pl.ds(at + 8, 8), :]
                    total = packed(total, value, v * CG + cl)
            pack[pl.ds(at, 8), :] = total
            return 0
        lax.fori_loop(0, chunks, body, 0, unroll=4)

    def operator(src, g, cl, at, ks, edges, first):
        q, d1, d2, out = [], {}, {}, []
        for v in range(NV):
            c = g * CG + cl
            mid = src[v, c, pl.ds(at + 8, 8), :]
            east = src[v, c, pl.ds(at + 9, 8), :]
            west = src[v, c, pl.ds(at + 7, 8), :]
            edge = pltpu.roll(edges, 127 - 2 * (v * CG + cl), 1)
            north = jnp.where(last_lane, edge, pltpu.roll(mid, 127, 1))
            south = jnp.where(first_lane, edge, pltpu.roll(mid, 1, 1))
            q.append(mid)
            if v in (1, 3):
                d1[v] = east - west
            if v in (2, 3):
                d2[v] = north - south
            out.append((ks[KE] * east + ks[KW] * west) + (ks[KN] * north + ks[KS] * south))
        for w in range(NV):
            m = [ks[KD + v if first and v == w else KM + w * NV + v] * q[v] for v in range(NV)]
            out[w] = out[w] + ((m[0] + m[1]) + (m[2] + m[3]))
        div = ks[KA] * (d1[1] + d2[2])
        out[0] = out[0] - div
        out[1] = out[1] - ks[KA] * d1[3]
        out[2] = out[2] - ks[KA] * d2[3]
        out[3] = out[3] - div
        return out

    def stage_one(g):
        def body(i, _):
            at = pl.multiple_of(i * 8, 8)
            ks = [coef[k, pl.ds(at, 8), :] for k in range(NK)]
            edges = halo[pl.ds(at, 8), :]
            total = jnp.zeros((8, 128), jnp.float32)
            for cl in range(CG):
                middle = operator(fbuf, g, cl, at, ks, edges, True)
                for v in range(NV):
                    mbuf[v, g * CG + cl, pl.ds(at + 8, 8), :] = middle[v]
                    total = packed(total, middle[v], v * CG + cl)
            pack[pl.ds(at, 8), :] = total
            return 0
        lax.fori_loop(0, chunks, body, 0, unroll=2)

    def stage_two(g):
        def body(i, _):
            at = pl.multiple_of(i * 8, 8)
            ks = [coef[k, pl.ds(at, 8), :] for k in range(NK)]
            edges = halo[pl.ds(at, 8), :]
            res = {}
            for cl in range(CG):
                c = g * CG + cl
                out = operator(mbuf, g, cl, at, ks, edges, False)
                for v in range(NV):
                    value = 1.5 * fbuf[v, c, pl.ds(at + 8, 8), :] + out[v]
                    rbuf[v, c, pl.ds(at, 8), :] = value
                    res[v, c] = value
            for c in range(g * CG):
                for v in range(NV):
                    res[v, c] = rbuf[v, c, pl.ds(at, 8), :]
            for c in range(g * CG, (g + 1) * CG):
                for d in range(c + 1):
                    p = [res[v, c] * res[v, d] for v in range(NV)]
                    acc[PAIR_INDEX[c, d]] += (p[0] + p[1]) + (p[2] + p[3])
            return 0
        lax.fori_loop(0, chunks, body, 0, unroll=2)

    def r_copy(g):
        return pltpu.make_async_copy(cols(rbuf, g), cols(r_hbm, g), out_sem.at[g])

    for g in range(GROUPS):
        loads[g].wait()
        pack_input(g)
        send(0, g, fbuf)
        if g == 0:
            pl.semaphore_wait(barrier, nx + ny - 2)
        launch(0, g)
    acc[...] = jnp.zeros_like(acc)
    for cp in coef_loads:
        cp.wait()

    def fold(i, _):
        at = pl.multiple_of(i * 8, 8)
        half = 0.5 * visc[pl.ds(at, 8), :]
        vx = 0.25 * vel[0, pl.ds(at, 8), :]
        vy = 0.25 * vel[1, pl.ds(at, 8), :]
        coef[KE, pl.ds(at, 8), :] = half - vx
        coef[KW, pl.ds(at, 8), :] = half + vx
        coef[KN, pl.ds(at, 8), :] = half - vy
        coef[KS, pl.ds(at, 8), :] = half + vy
        coef[KA, pl.ds(at, 8), :] = 0.25 * sound[pl.ds(at, 8), :]
        for w in range(NV):
            for v in range(NV):
                k = -0.5 * coup[w, v, pl.ds(at, 8), :]
                if v == w:
                    coef[KD + v, pl.ds(at, 8), :] = k + (1.5 - 4.0 * half)
                    k = k + (1.0 - 4.0 * half)
                coef[KM + w * NV + v, pl.ds(at, 8), :] = k
        return 0
    lax.fori_loop(0, chunks, fold, 0, unroll=2)

    for g in range(GROUPS):
        receive(0, g, fbuf)
        stage_one(g)
        send(1, g, mbuf)
        launch(1, g)
    for g in range(GROUPS):
        receive(1, g, mbuf)
        stage_two(g)
        r_copy(g).start()

    scale = 0.25 / float(NV * rows * 128 * nx * ny)
    lanes = jnp.sum(jnp.sum(acc[...], axis=1), axis=1, keepdims=True)
    spot = lax.broadcasted_iota(jnp.int32, (PADDED_PAIRS, 128), 1) == lax.broadcasted_iota(
        jnp.int32, (PADDED_PAIRS, 128), 0)
    line = jnp.sum(jnp.where(spot, lanes, 0.0), axis=0, keepdims=True) * scale
    gx_slots[gx] = jnp.broadcast_to(line, (8, 128))

    def gx_copy(r, owner):
        return pltpu.make_async_remote_copy(
            src_ref=gx_slots.at[owner], dst_ref=gx_slots.at[owner],
            send_sem=g1_send.at[r], recv_sem=g1_recv.at[owner],
            device_id=(lax.rem(gx + r, nx), gy), device_id_type=MESH)

    def gy_copy(r, owner):
        return pltpu.make_async_remote_copy(
            src_ref=gy_slots.at[owner], dst_ref=gy_slots.at[owner],
            send_sem=g2_send.at[r], recv_sem=g2_recv.at[owner],
            device_id=(gx, lax.rem(gy + r, ny)), device_id_type=MESH)

    for r in range(1, nx):
        gx_copy(r, gx).start()
    for r in range(1, nx):
        gx_copy(r, lax.rem(gx + nx - r, nx)).wait_recv()
    gy_slots[gy] = functools.reduce(jnp.add, [gx_slots[k] for k in range(nx)])
    for r in range(1, ny):
        gy_copy(r, gy).start()
    for r in range(1, ny):
        gy_copy(r, lax.rem(gy + ny - r, ny)).wait_recv()
    gram_ref[...] = functools.reduce(jnp.add, [gy_slots[k] for k in range(ny)])

    for r in range(1, nx):
        gx_copy(r, gx).wait_send()
    for r in range(1, ny):
        gy_copy(r, gy).wait_send()
    for s in range(2):
        for g in range(GROUPS):
            finish_sends(s, g)
    for g in range(GROUPS):
        r_copy(g).wait()


def basis_kernel(gram_ref, r_ref, basis_hbm, factor_ref, inv_ref, basis_ref, out_sem):
    def factorise():
        gram = {p: jnp.broadcast_to(gram_ref[:, k:k + 1], (8, 128)) for k, p in enumerate(PAIRS)}
        low, inv, diag = {}, {}, {}
        for j in range(NC):
            for i in range(j, NC):
                s = gram[i, j]
                for k in range(j):
                    s = s - low[i, k] * low[j, k]
                if i == j:
                    r = lax.rsqrt(s)
                    r = r * (1.5 - 0.5 * s * r * r)
                    diag[j] = r
                    low[j, j] = s * r
                else:
                    low[i, j] = s * diag[j]
        for j in range(NC):
            inv[j, j] = diag[j]
            for i in range(j + 1, NC):
                s = low[i, j] * inv[j, j]
                for k in range(j + 1, i):
                    s = s + low[i, k] * inv[k, j]
                inv[i, j] = -diag[i] * s
        row = lax.broadcasted_iota(jnp.int32, (8, 128), 0)
        lane = lax.broadcasted_iota(jnp.int32, (8, 128), 1)
        factor = jnp.zeros((8, 128), jnp.float32)
        for k, (i, j) in enumerate(PAIRS):
            factor = jnp.where((row == j) & (lane == i), low[i, j], factor)
            inv_ref[k] = 0.5 * inv[i, j]
        factor_ref[...] = factor[:, :NC]

    factorise()
    inv = [inv_ref[k] for k in range(len(PAIRS))]

    def out_copy(v):
        return pltpu.make_async_copy(basis_ref.at[v], basis_hbm.at[v], out_sem.at[v])

    for v in range(NV):
        def body(i, _):
            at = pl.multiple_of(i * 8, 8)
            r = [r_ref[v, c, pl.ds(at, 8), :] for c in range(NC)]
            for c in range(NC):
                total = inv[PAIR_INDEX[c, 0]] * r[0]
                for d in range(1, c + 1):
                    total = total + inv[PAIR_INDEX[c, d]] * r[d]
                basis_ref[v, c, pl.ds(at, 8), :] = total
            return 0
        lax.fori_loop(0, r_ref.shape[2] // 8, body, 0, unroll=2)
        out_copy(v).start()
    for v in range(NV):
        out_copy(v).wait()


def local(nx, ny, forcing, velocity, viscosity, sound, coupling):
    rows = forcing.shape[2]
    f32 = jnp.float32
    hbm = pl.BlockSpec(memory_space=pl.ANY)
    vmem = pl.BlockSpec(memory_space=pltpu.VMEM)
    dma = pltpu.SemaphoreType.DMA
    response, gram = pl.pallas_call(
        functools.partial(response_kernel, nx, ny),
        out_shape=(jax.ShapeDtypeStruct(forcing.shape, f32), jax.ShapeDtypeStruct((8, 128), f32)),
        in_specs=[pl.BlockSpec(memory_space=pltpu.HBM)] * 5,
        out_specs=(hbm, vmem),
        scratch_shapes=[
            pltpu.VMEM((NV, NC, rows + 16, 128), f32),
            pltpu.VMEM((NV, NC, rows + 16, 128), f32),
            pltpu.VMEM((NV, NC, rows, 128), f32),
            pltpu.VMEM((NK, rows, 128), f32),
            pltpu.VMEM((rows, 128), f32),
            pltpu.VMEM((rows, 128), f32),
            pltpu.VMEM((128, 128), f32),
            pltpu.VMEM(velocity.shape, f32),
            pltpu.VMEM(viscosity.shape, f32),
            pltpu.VMEM(sound.shape, f32),
            pltpu.VMEM(coupling.shape, f32),
            pltpu.VMEM((PADDED_PAIRS, 8, 128), f32),
            pltpu.VMEM((nx, 8, 128), f32),
            pltpu.VMEM((ny, 8, 128), f32),
            pltpu.VMEM((2, GROUPS, 2, NF, 128), f32),
            pltpu.VMEM((2, GROUPS, 2, NF, 128), f32),
            pltpu.VMEM((2, GROUPS, 2, rows // 128 * NF, 128), f32),
            pltpu.VMEM((2, GROUPS, 2, rows // 128 * NF, 128), f32),
            dma((GROUPS + 4,)), dma((GROUPS,)),
            dma((2, GROUPS, 2)), dma((2, GROUPS, 2)), dma((2, GROUPS, 2)), dma((2, GROUPS, 2)),
            dma((nx,)), dma((nx,)), dma((ny,)), dma((ny,)),
        ],
        compiler_params=pltpu.CompilerParams(
            collective_id=0, has_side_effects=True, vmem_limit_bytes=40 * 2**20),
        name="response",
    )(*[pltpu.with_memory_space_constraint(a, pltpu.HBM)
        for a in (forcing, velocity, viscosity, sound, coupling)])
    return tuple(pl.pallas_call(
        basis_kernel,
        out_shape=(jax.ShapeDtypeStruct(forcing.shape, f32), jax.ShapeDtypeStruct((NC, NC), f32)),
        in_specs=[vmem, vmem],
        out_specs=(hbm, vmem),
        scratch_shapes=[
            pltpu.VMEM((len(PAIRS), 8, 128), f32),
            pltpu.VMEM(forcing.shape, f32),
            dma((NV,)),
        ],
        compiler_params=pltpu.CompilerParams(vmem_limit_bytes=16 * 2**20),
        name="basis",
    )(gram, response))


def solution(mesh):
    in_specs = (
        P(None, None, "gx", "gy"),
        P(None, "gx", "gy"),
        P("gx", "gy"),
        P("gx", "gy"),
        P(None, None, "gx", "gy"),
    )
    out_specs = (P(None, None, "gx", "gy"), P())
    body = functools.partial(local, mesh.shape["gx"], mesh.shape["gy"])
    return jax.shard_map(body, mesh=mesh, in_specs=in_specs, out_specs=out_specs, check_vma=False)
```
